32 devices in a mesh: segment: 8 (over z, core), head: 4 (over y, x).
Axes of the slice: x: 2, y: 2, z: 4, core: 2. Of those that a mesh axis runs over, the one named last changes fastest.
Arguments:
- slices: bfloat16 [1024, 4096], P('segment', 'head'), may hold values from -6 to 6
- new_slice: bfloat16 [128, 4096], P(None, 'head'), may hold values from -6 to 6
- norm_gain: float32 [8, 4096], P('segment'), may hold values from 0.1 to 1.9
- w_query: bfloat16 [8, 4096, 2048], P('segment', None, 'head'), may hold values from -0.09375 to 0.09375
- w_keyval: bfloat16 [8, 4096, 1024], P('segment', None, 'head'), may hold values from -0.1875 to 0.1875
- w_out: bfloat16 [8, 2048, 4096], P('segment', 'head'), may hold values from -0.375 to 0.375
- cached_rows: bfloat16 [8, 16384, 256], P('segment', 'head'), may hold values from -400 to 400
- lengths: int32 [8], P('segment'), may hold values from 256 to 4096
Outputs:
- first_pass: float32 [1024, 4096], P('segment', 'head')
- second_pass: float32 [1024, 4096], P('segment', 'head')
The draws below stay inside these ranges and needn't reach their ends.
All inputs are finite; a program needn't handle non-finite values.
Results may differ from the reference program's by a relative error of at most 0.029.
The reference program's roundings to bfloat16 on the way (of `normed`, `queries`, `weights` and `attended`) count: a program that leaves them out, or rounds other values in their place, can miss the bound.
Values may be sent and summed in bfloat16 or wider, within the bound.
A program may use at most 64 MiB of HBM per device.

```python
import jax
import jax.numpy as jnp
from jax import lax

D = 4096
H = 16
KVH = 4
HD = 128
ROWS = 128
CMAX = 4096
SEGMENTS = 8
N_SEGMENT = 8


def draw_cached_rows(key, part):
    base_key = jax.random.fold_in(key, 101)
    shape = (SEGMENTS, KVH, CMAX, 2 * HD)
    base = jnp.clip(2.0 * jax.random.normal(base_key, shape, jnp.float32), -12.0, 12.0)
    return base.reshape(SEGMENTS, KVH * CMAX, 2 * HD).astype(jnp.bfloat16)


def plant(drawn, own_key, smallest, top_value):
    shape = drawn.shape
    spot = [jax.random.randint(jax.random.fold_in(own_key, axis), (), 0, shape[axis]) for axis in range(len(shape))]
    drawn = drawn.at[tuple(spot)].set(smallest)
    longest = shape.index(max(shape))
    spot[longest] = (spot[longest] + 1) % shape[longest]
    return drawn.at[tuple(spot)].set(top_value)


def spiked(values, stream_key, source, target, parts, factor):
    owner, partner = [(jnp.arange(values.shape[axis_at]) // (values.shape[axis_at] // parts)).reshape([-1 if axis == axis_at else 1 for axis in range(values.ndim)]) for axis_at in (source, target)]
    chosen = jax.random.permutation(stream_key, parts)[partner]
    strong = (owner == chosen) | (owner == (partner + parts // 2) % parts)
    return jnp.where(strong, factor * values, values)


def block_levels(rng, dims, split, smallest, largest):
    def one(dim, shards_of):
        draws = jax.random.uniform(jax.random.fold_in(jax.random.fold_in(rng, 6), dim), (shards_of,), jnp.float32, smallest / len(split), largest / len(split))
        return jnp.repeat(jnp.exp(draws), dims[dim] // shards_of).reshape((-1,) + (1,) * (len(dims) - dim - 1))

    factor_of = one(*split[0])
    for cut in split[1:]:
        factor_of = factor_of * one(*cut)
    return factor_of


def scatter_about(stream_key, extent, spread, reach, cuts=(), kind=jnp.bfloat16):
    values = spread * jax.random.normal(stream_key, extent, jnp.float32)
    if cuts:
        values = values * block_levels(stream_key, extent, cuts, -0.22, 0.18)
    return jnp.clip(values, -reach, reach).astype(kind)


def heavy_noise(rng, extent, deviation, most, pieces, heavy, kind=jnp.bfloat16):
    values = deviation * jax.random.normal(rng, extent, jnp.float32)
    if pieces:
        values = values * block_levels(rng, extent, pieces, -0.22, 0.18)
    return jnp.clip(spiked(values, jax.random.fold_in(rng, 3), *heavy), -most, most).astype(kind)


def setup_inputs(seed: int = 0) -> dict:
    key_list = jax.random.split(jax.random.key(seed), 9)
    slices = scatter_about(key_list[0], (SEGMENTS * ROWS, D), 1.0, 6.0, ((0, 8), (1, 4)))
    new_slice = scatter_about(key_list[1], (ROWS, D), 1.0, 6.0, ((1, 4),))
    norm_gain = jnp.clip(1.0 + 0.18 * jax.random.normal(key_list[2], (SEGMENTS, D), jnp.float32), 0.1, 1.9)
    w_query = scatter_about(key_list[3], (SEGMENTS, D, H * HD), D ** -0.5, 0.09375, ((0, 8), (2, 4)))
    w_keyval = scatter_about(key_list[4], (SEGMENTS, D, 2 * KVH * HD), (D // 4) ** -0.5, 0.1875, ((0, 8), (2, 4)))
    w_out = heavy_noise(key_list[5], (SEGMENTS, H * HD, D), (H * HD // 4) ** -0.5, 0.375, ((0, 8), (1, 4)), (1, 2, 4, 2.0))
    cached_rows = draw_cached_rows(jax.random.fold_in(key_list[8], 71), 0)
    lengths = plant(jax.random.randint(key_list[7], (SEGMENTS,), CMAX // 16, CMAX + 1), jax.random.fold_in(key_list[7], 1), CMAX // 16, CMAX).astype(jnp.int32)
    return {"slices": slices, "new_slice": new_slice, "norm_gain": norm_gain, "w_query": w_query, "w_keyval": w_keyval, "w_out": w_out, "cached_rows": cached_rows, "lengths": lengths}


EPSILON = 1e-05
ROPE_BASE = 1000000.0
NEGATIVE = -1e+30

def rotate(entries, positions):
    half_dim = entries.shape[-1] // 2
    exponent = jnp.arange(half_dim, dtype=jnp.float32) * (2.0 / entries.shape[-1])
    inverse = jnp.power(jnp.float32(ROPE_BASE), -exponent)
    angles = positions[:, None] * inverse[None, :]
    cosine = jnp.cos(angles)[:, None, :]
    sine = jnp.sin(angles)[:, None, :]
    first_half = entries[..., :half_dim]
    second_half = entries[..., half_dim:]
    return jnp.concatenate([first_half * cosine - second_half * sine, second_half * cosine + first_half * sine], axis=-1)

def normalize(rows_in, gain_vector):
    widened = rows_in.astype(jnp.float32)
    mean_square = lax.optimization_barrier(jnp.mean(widened * widened, axis=-1, keepdims=True))
    return (widened * lax.rsqrt(mean_square + EPSILON) * gain_vector).astype(jnp.bfloat16)

def section(rows_in, gain_vector, query_w, keyval_w, out_w, cache_part, length, offset, earlier_keys, earlier_values, earlier_live):
    row_count = rows_in.shape[0]
    normed = normalize(rows_in, gain_vector)
    positions = (length + offset + jnp.arange(row_count, dtype=jnp.int32)).astype(jnp.float32)
    queries = jnp.dot(normed, query_w, preferred_element_type=jnp.float32).reshape(row_count, H, HD)
    queries = rotate(queries, positions).astype(jnp.bfloat16)
    projected = jnp.dot(normed, keyval_w, preferred_element_type=jnp.float32).reshape(row_count, KVH, 2, HD)
    new_keys = rotate(projected[:, :, 0], positions).astype(jnp.bfloat16)
    new_values = projected[:, :, 1].astype(jnp.bfloat16)
    group_size = H // KVH
    cache_table = cache_part.reshape(KVH, CMAX, 2 * HD)
    cache_live = jnp.arange(CMAX, dtype=jnp.int32) < length
    row_ids = jnp.arange(row_count, dtype=jnp.int32)
    causal = row_ids[:, None] >= row_ids[None, :]
    visible = jnp.concatenate([jnp.broadcast_to(cache_live[None, :], (row_count, CMAX)), jnp.broadcast_to(jnp.asarray(earlier_live), (row_count, row_count)), causal], axis=1)
    scaling = HD ** (-0.5)

    def attend(operands):
        head_queries, cache_rows, fresh_keys, fresh_values, old_keys, old_values = operands
        key_rows = jnp.concatenate([cache_rows[:, :HD], old_keys, fresh_keys], axis=0).astype(jnp.float32)
        value_rows = jnp.concatenate([cache_rows[:, HD:], old_values, fresh_values], axis=0).astype(jnp.float32)
        scores = jnp.einsum('rgd,kd->grk', head_queries.astype(jnp.float32), key_rows) * scaling
        scores = jnp.where(visible[None], scores, NEGATIVE)
        row_peak = lax.optimization_barrier(jnp.max(scores, axis=-1, keepdims=True))
        weights = jnp.where(visible[None], jnp.exp(scores - row_peak), 0.0)
        row_total = lax.optimization_barrier(jnp.sum(weights, axis=-1, keepdims=True))
        rounded = weights.astype(jnp.bfloat16)
        summed = jnp.einsum('grk,kd->grd', rounded.astype(jnp.float32), value_rows)
        return (summed / row_total).transpose(1, 0, 2).astype(jnp.bfloat16)
    operands = (queries.reshape(row_count, KVH, group_size, HD).transpose(1, 0, 2, 3), cache_table, new_keys.transpose(1, 0, 2), new_values.transpose(1, 0, 2), earlier_keys.transpose(1, 0, 2), earlier_values.transpose(1, 0, 2))
    attended = lax.map(attend, operands).transpose(1, 0, 2, 3).reshape(row_count, H * HD)
    mixed = jnp.dot(attended, out_w, preferred_element_type=jnp.float32)
    result = rows_in.astype(jnp.float32) + mixed
    return (result, new_keys, new_values)

def reference(slices, new_slice, norm_gain, w_query, w_keyval, w_out, cached_rows, lengths):
    stacked = slices.astype(jnp.float32).reshape(N_SEGMENT, ROWS, D)
    blank_rows = jnp.zeros((ROWS, KVH, HD), jnp.bfloat16)

    def first_turn(operands):
        rows_in, gain_vector, query_w, keyval_w, out_w, cache_part, length = operands
        return section(rows_in, gain_vector, query_w, keyval_w, out_w, cache_part, length, 0, blank_rows, blank_rows, False)
    first_out, saved_keys, saved_values = lax.map(first_turn, (stacked, norm_gain, w_query, w_keyval, w_out, cached_rows, lengths))
    entering = jnp.concatenate([new_slice.astype(jnp.float32)[None], first_out[:-1]], axis=0)

    def second_turn(operands):
        rows_in, gain_vector, query_w, keyval_w, out_w, cache_part, length, old_keys, old_values = operands
        result, _, _ = section(rows_in, gain_vector, query_w, keyval_w, out_w, cache_part, length, ROWS, old_keys, old_values, True)
        return result
    second_out = lax.map(second_turn, (entering, norm_gain, w_query, w_keyval, w_out, cached_rows, lengths, saved_keys, saved_values))
    return (first_out.reshape(N_SEGMENT * ROWS, D), second_out.reshape(N_SEGMENT * ROWS, D))
```

```python
import functools

import jax
import jax.numpy as jnp
from jax import lax
from jax.experimental import pallas as pl
from jax.experimental.pallas import tpu as pltpu
from jax.sharding import PartitionSpec as P

KVH = 4
HD = 128
MESH = pl.DeviceIdType.MESH


EPSILON = 1e-05
ROPE_BASE = 1000000.0
NEGATIVE = -1e30


def swapped(block, axis, bit):
    count = lax.axis_size(axis)
    route = []
    for low in range(count):
        high = low | 1 << bit
        if high != low and high < count:
            route += [(low, high), (high, low)]
    return lax.ppermute(block, axis, route)


def from_behind(shard, axis, by):
    peers = lax.axis_size(axis)
    pairs = [(i, i + by) for i in range(peers) if 0 <= i + by < peers]
    return lax.ppermute(shard, axis, pairs)


def rotate(entries, positions):
    half_dim = entries.shape[-1] // 2
    exponent = jnp.arange(half_dim, dtype=jnp.float32) * (2.0 / entries.shape[-1])
    inverse = jnp.power(jnp.float32(ROPE_BASE), -exponent)
    angles = positions[:, None] * inverse[None, :]
    cosine = jnp.cos(angles)[:, None, :]
    sine = jnp.sin(angles)[:, None, :]
    first_half = entries[..., :half_dim]
    second_half = entries[..., half_dim:]
    return jnp.concatenate(
        [first_half * cosine - second_half * sine, second_half * cosine + first_half * sine],
        axis=-1,
    )


def normalize(rows_in, gain_vector):
    mean_square = jnp.mean(rows_in * rows_in, axis=-1, keepdims=True)
    return (rows_in * lax.rsqrt(mean_square + EPSILON) * gain_vector).astype(jnp.bfloat16)


def combine_partial(left_side, right_side):
    left_peak, left_total, left_out = left_side
    right_peak, right_total, right_out = right_side
    joined = jnp.maximum(left_peak, right_peak)
    left_scale = jnp.exp(left_peak - joined)
    right_scale = jnp.exp(right_peak - joined)
    return (
        joined,
        left_scale * left_total + right_scale * right_total,
        left_scale[..., None] * left_out + right_scale[..., None] * right_out,
    )


def softmax_partial(queries, key_rows, value_rows, visible):
    scores = jnp.einsum(
        "rnd,kd->nrk", queries, key_rows, preferred_element_type=jnp.float32
    ) * HD ** (-0.5)
    scores = jnp.where(visible[None], scores, NEGATIVE)
    row_peak = jnp.max(scores, axis=-1)
    weights = jnp.where(visible[None], jnp.exp(scores - row_peak[..., None]), 0.0)
    row_total = jnp.sum(weights, axis=-1)
    outputs = jnp.einsum(
        "nrk,kd->nrd", weights.astype(jnp.bfloat16), value_rows, preferred_element_type=jnp.float32
    )
    return (row_peak, row_total, outputs)


def blank_partial(head_total, row_total):
    return (
        jnp.full((head_total, row_total), NEGATIVE, jnp.float32),
        jnp.zeros((head_total, row_total), jnp.float32),
        jnp.zeros((head_total, row_total, HD), jnp.float32),
    )


def attend_range(query_set, key_table, low_bound, high_bound, block_rows):
    row_total = query_set.shape[0]
    first_block = low_bound // block_rows
    last_block = (high_bound + block_rows - 1) // block_rows

    def one_block(turn_index, running):
        block_start = (first_block + turn_index) * block_rows
        key_piece = lax.dynamic_slice_in_dim(key_table, block_start, block_rows, 0)
        places = block_start + jnp.arange(block_rows, dtype=jnp.int32)
        live_mask = (places >= low_bound) & (places < high_bound)
        visible = jnp.broadcast_to(live_mask[None, :], (row_total, block_rows))
        return combine_partial(
            running, softmax_partial(query_set, key_piece[:, :HD], key_piece[:, HD:], visible)
        )

    turns = jnp.maximum(last_block - first_block, 0)
    return lax.fori_loop(0, turns, one_block, blank_partial(query_set.shape[1], row_total))


def local(slices, new_slice, norm_gain, w_query, w_keyval, w_out, cached_rows, lengths):
    segment_index = lax.axis_index("segment")
    head_index = lax.axis_index("head")
    head_count = lax.axis_size("head")
    row_count, width = slices.shape
    group_size = head_count // KVH
    bit_count = group_size.bit_length() - 1
    position = head_index % group_size
    local_heads = w_query.shape[2] // HD
    length = lengths[0]
    gain_vector = norm_gain[0]
    query_w = w_query[0]
    keyval_w = w_keyval[0]
    out_w = w_out[0]
    cache_rows = cached_rows[0]
    row_ids = jnp.arange(row_count, dtype=jnp.int32)
    causal = row_ids[:, None] >= row_ids[None, :]
    assembled = cache_rows
    for bit_number in range(bit_count):
        partner_rows = swapped(assembled, "head", bit_number)
        high_bit = position // (1 << bit_number) % 2
        assembled = jnp.where(
            high_bit == 0,
            jnp.concatenate([assembled, partner_rows], axis=0),
            jnp.concatenate([partner_rows, assembled], axis=0),
        )
    table_rows = assembled.shape[0]
    block_rows = min(512, table_rows // 4)
    own_live = jnp.clip(length, 0, table_rows)

    def cache_partial(query_set):
        combined = attend_range(query_set, assembled, 0, own_live, block_rows)
        return combined

    def project(full_rows, offset):
        normed = normalize(full_rows, gain_vector)
        positions = (length + offset + row_ids).astype(jnp.float32)
        queries = jnp.dot(normed, query_w, preferred_element_type=jnp.float32).reshape(
            row_count, local_heads, HD
        )
        queries = rotate(queries, positions).astype(jnp.bfloat16)
        chosen = jnp.dot(normed, keyval_w, preferred_element_type=jnp.float32)
        for bit_number in range(bit_count):
            partner_part = swapped(chosen, "head", bit_number)
            high_bit = position // (1 << bit_number) % 2
            chosen = jnp.where(
                high_bit == 0,
                jnp.concatenate([chosen, partner_part], axis=1),
                jnp.concatenate([partner_part, chosen], axis=1),
            )
        new_keys = rotate(chosen[:, None, :HD], positions)[:, 0].astype(jnp.bfloat16)
        new_values = chosen[:, HD:].astype(jnp.bfloat16)
        return (queries, new_keys, new_values)

    def attend(queries, new_keys, new_values, earlier):
        if earlier is None:
            recent_keys = new_keys
            recent_values = new_values
            recent_live = causal
        else:
            recent_keys = jnp.concatenate([earlier[0], new_keys], axis=0)
            recent_values = jnp.concatenate([earlier[1], new_values], axis=0)
            recent_live = jnp.concatenate([jnp.ones((row_count, row_count), bool), causal], axis=1)
        running = cache_partial(queries)
        recent = softmax_partial(queries, recent_keys, recent_values, recent_live)
        row_peak, row_total, outputs = combine_partial(running, recent)
        attended = (outputs / row_total[..., None]).astype(jnp.bfloat16).transpose(1, 0, 2)
        return attended.reshape(row_count, local_heads * HD)

    def mix(full_rows, offset, earlier):
        queries, new_keys, new_values = project(full_rows, offset)
        attended = attend(queries, new_keys, new_values, earlier)
        return (
            jnp.dot(attended, out_w, preferred_element_type=jnp.float32),
            (new_keys, new_values),
        )

    def advance(own_rows, offset, earlier):
        full_rows = lax.all_gather(own_rows, "head", axis=1, tiled=True)
        partial_out, recent = mix(full_rows, offset, earlier)
        summed = lax.psum_scatter(partial_out, "head", scatter_dimension=1, tiled=True)
        return (own_rows + summed, recent)

    first_out, recent = advance(slices.astype(jnp.float32), 0, None)
    arrived = from_behind(first_out, "segment", 1)
    entering = jnp.where(segment_index == 0, new_slice.astype(jnp.float32), arrived)
    second_out, _ = advance(entering, row_count, recent)
    return (first_out, second_out)


def exchange_kernel(
    row_chunks, x_ref, new_ref, gain_ref, cos_ref, sin_ref, len_ref, wq_hbm, wkv_hbm, wo_hbm, cache_hbm,
    first_ref, second_ref,
    wq, wkv, wo, cache, gathered, normed, q_buf, score_buf, mask_buf, new_k, new_v, att_buf,
    diag_send, x_send, y_send, keep_x, keep_y, keep_own, diag_x_land, diag_y_land, x_land, y_land,
    forward_buf, load_sem, send_sem, recv_sem,
):
    seg = lax.axis_index("segment")
    me = lax.axis_index("head")
    seg_count = lax.axis_size("segment")
    x_peer = me + 1 - 2 * (me % 2)
    y_peer = (me + 2) % 4
    far_peer = x_peer + 2 - 4 * (x_peer // 2)
    rows, features = x_ref.shape
    blocks = gathered.shape[1]
    chunk = rows // row_chunks
    half = chunk // 2
    local_heads = wq.shape[1] // HD
    cached = cache.shape[0]
    key_block = min(512, cached)
    exponent_scale = HD ** (-0.5) * 1.4426950408889634

    loads = [
        pltpu.make_async_copy(source, target, load_sem.at[i])
        for i, (source, target) in enumerate(
            [(wq_hbm.at[0], wq), (wkv_hbm.at[0], wkv), (cache_hbm.at[0], cache), (wo_hbm.at[0], wo)]
        )
    ]
    for load in loads:
        load.start()

    gathered[0, me] = x_ref[...]

    barrier = pltpu.get_barrier_semaphore()
    for peer in (x_peer, y_peer):
        pl.semaphore_signal(barrier, inc=1, device_id={"head": peer}, device_id_type=MESH)

    @pl.when(seg > 0)
    def _():
        pl.semaphore_signal(barrier, inc=1, device_id={"segment": seg - 1}, device_id_type=MESH)

    @pl.when(seg < seg_count - 1)
    def _():
        pl.semaphore_signal(barrier, inc=1, device_id={"segment": seg + 1}, device_id_type=MESH)

    before = (seg + seg_count - 1) // seg_count
    after = (2 * seg_count - 2 - seg) // seg_count
    pl.semaphore_wait(barrier, 2 + before + after)

    copies = []

    def remote(source, target, where):
        at = len(copies)
        made = pltpu.make_async_remote_copy(
            src_ref=source, dst_ref=target, send_sem=send_sem.at[at], recv_sem=recv_sem.at[at],
            device_id=where, device_id_type=MESH,
        )
        copies.append(made)
        return made

    def low(c):
        return pl.ds(c * chunk, half)

    def high(c):
        return pl.ds(c * chunk + half, half)

    gather_copies = {}

    def gather_send(p, c):
        made = []
        for part in (low(c), high(c)):
            own = gathered.at[p, me, part]
            made.append(remote(own, own, {"head": x_peer}))
        for part in (high(c), low(c)):
            own = gathered.at[p, me, part]
            made.append(remote(own, own, {"head": y_peer}))
        gather_copies[p, c] = made
        for at in (0, 2, 1, 3):
            made[at].start()

    def gather_pass_on(p, c):
        made = gather_copies[p, c]
        made[0].wait_recv()
        from_x = gathered.at[p, x_peer, low(c)]
        made.append(remote(from_x, from_x, {"head": y_peer}))
        made[4].start()
        made[2].wait_recv()
        from_y = gathered.at[p, y_peer, high(c)]
        made.append(remote(from_y, from_y, {"head": x_peer}))
        made[5].start()

    def rope(entries, table_rows):
        return entries * cos_ref[table_rows] + pltpu.roll(entries, HD // 2, 1) * sin_ref[table_rows]

    def project(p, c):
        made = gather_copies[p, c]
        for at in (1, 3, 4, 5):
            made[at].wait_recv()
        part = pl.ds(c * chunk, chunk)
        total = jnp.zeros((chunk, 1), jnp.float32)
        for b in range(blocks):
            piece = gathered[p, b, part].astype(jnp.float32)
            total = total + jnp.sum(piece * piece, axis=-1, keepdims=True)
        scale = lax.rsqrt(total / (blocks * features) + EPSILON)
        for b in range(blocks):
            piece = gathered[p, b, part].astype(jnp.float32)
            columns = pl.ds(b * features, features)
            normed[:, columns] = (piece * scale * gain_ref[:, columns]).astype(jnp.bfloat16)
        table_rows = pl.ds(p * rows + c * chunk, chunk)
        if p == 0 and c == 0:
            loads[0].wait()
            loads[1].wait()
        queries = jnp.dot(normed[...], wq[...], preferred_element_type=jnp.float32)
        for j in range(local_heads):
            turned = rope(queries[:, j * HD:(j + 1) * HD], table_rows)
            q_buf[pl.ds(j * chunk, chunk)] = turned.astype(jnp.bfloat16)
        chosen = jnp.dot(normed[...], wkv[...], preferred_element_type=jnp.float32)
        new_k[p, part] = rope(chosen[:, :HD], table_rows).astype(jnp.bfloat16)
        new_v[p, part] = chosen[:, HD:].astype(jnp.bfloat16)

    def attend(p, c):
        if p == 0 and c == 0:
            loads[2].wait()
        queries = q_buf[...]
        count = local_heads * chunk

        def product(keys):
            return lax.dot_general(
                queries, keys, (((1,), (1,)), ((), ())), preferred_element_type=jnp.float32
            )

        peak = jnp.full((count, HD), NEGATIVE, jnp.float32)
        for start in range(0, cached, key_block):
            scores = product(cache[pl.ds(start, key_block), pl.ds(0, HD)])
            scores = scores + mask_buf[:, pl.ds(start, key_block)]
            score_buf[:, pl.ds(start, key_block)] = scores
            for lane in range(0, key_block, HD):
                peak = jnp.maximum(peak, scores[:, lane:lane + HD])
        recents = []
        for earlier in range(p):
            recents.append((product(new_k[earlier]), earlier))
        scores = product(new_k[p])
        row_at = lax.broadcasted_iota(jnp.int32, scores.shape, 0) % chunk + c * chunk
        key_at = lax.broadcasted_iota(jnp.int32, scores.shape, 1)
        recents.append((jnp.where(key_at <= row_at, scores, NEGATIVE), p))
        for scores, _ in recents:
            peak = jnp.maximum(peak, scores)
        top = jnp.max(peak, axis=-1, keepdims=True)
        sums = jnp.zeros((count, HD), jnp.float32)
        outputs = jnp.zeros((count, HD), jnp.float32)
        for scores, which in recents:
            weights = jnp.exp2((scores - top) * exponent_scale)
            sums = sums + weights
            outputs = outputs + jnp.dot(
                weights.astype(jnp.bfloat16), new_v[which], preferred_element_type=jnp.float32
            )
        for start in range(0, cached, key_block):
            weights = jnp.exp2((score_buf[:, pl.ds(start, key_block)] - top) * exponent_scale)
            for lane in range(0, key_block, HD):
                sums = sums + weights[:, lane:lane + HD]
            outputs = outputs + jnp.dot(
                weights.astype(jnp.bfloat16), cache[pl.ds(start, key_block), pl.ds(HD, HD)],
                preferred_element_type=jnp.float32,
            )
        attended = (outputs / jnp.sum(sums, axis=-1, keepdims=True)).astype(jnp.bfloat16)
        for j in range(local_heads):
            att_buf[:, pl.ds(j * HD, HD)] = attended[j * chunk:(j + 1) * chunk]

    scatter_copies = {}

    def mix(p, c):
        if p == 0 and c == 0:
            loads[3].wait()
        part = pl.ds(c * chunk, chunk)

        def partial(owner):
            columns = pl.ds(pl.multiple_of(owner * features, features), features)
            return jnp.dot(att_buf[...], wo[:, columns], preferred_element_type=jnp.float32)

        diag_send[p, part] = partial(far_peer).astype(jnp.bfloat16)
        made = [
            remote(diag_send.at[p, low(c)], diag_x_land.at[p, c], {"head": x_peer}),
            remote(diag_send.at[p, high(c)], diag_y_land.at[p, c], {"head": y_peer}),
        ]
        made[0].start()
        made[1].start()
        for_x = partial(x_peer)
        x_send[p, low(c)] = for_x[:half].astype(jnp.bfloat16)
        keep_x[c] = for_x[half:]
        made.append(remote(x_send.at[p, low(c)], x_land.at[p, low(c)], {"head": x_peer}))
        made[2].start()
        for_y = partial(y_peer)
        y_send[p, high(c)] = for_y[half:].astype(jnp.bfloat16)
        keep_y[c] = for_y[:half]
        made.append(remote(y_send.at[p, high(c)], y_land.at[p, high(c)], {"head": y_peer}))
        made[3].start()
        keep_own[part] = partial(me)
        scatter_copies[p, c] = made

    def combine(p, c):
        made = scatter_copies[p, c]
        made[0].wait_recv()
        y_send[p, low(c)] = (keep_y[c] + diag_x_land[p, c].astype(jnp.float32)).astype(jnp.bfloat16)
        made.append(remote(y_send.at[p, low(c)], y_land.at[p, low(c)], {"head": y_peer}))
        made[4].start()
        made[1].wait_recv()
        x_send[p, high(c)] = (keep_x[c] + diag_y_land[p, c].astype(jnp.float32)).astype(jnp.bfloat16)
        made.append(remote(x_send.at[p, high(c)], x_land.at[p, high(c)], {"head": x_peer}))
        made[5].start()

    def finish(p, c):
        made = scatter_copies[p, c]
        for at in (2, 3, 4, 5):
            made[at].wait_recv()
        part = pl.ds(c * chunk, chunk)
        arrived = x_land[p, part].astype(jnp.float32) + y_land[p, part].astype(jnp.float32)
        return gathered[p, me, part].astype(jnp.float32) + (keep_own[part] + arrived)

    forward_copies = {}

    def finish_first(c):
        part = pl.ds(c * chunk, chunk)
        result = finish(0, c)
        first_ref[part] = result
        forward_buf[part] = result.astype(jnp.bfloat16)
        made = remote(forward_buf.at[part], gathered.at[1, me, part], {"segment": seg + 1})
        forward_copies[c] = made

        @pl.when(seg < seg_count - 1)
        def _():
            made.start()

    def enter(c):
        @pl.when(seg > 0)
        def _():
            forward_copies[c].wait_recv()

        gather_send(1, c)

    def finish_second(c):
        second_ref[pl.ds(c * chunk, chunk)] = finish(1, c)

    for c in range(row_chunks):
        gather_send(0, c)

    @pl.when(seg == 0)
    def _():
        gathered[1, me] = new_ref[...]

    place = lax.broadcasted_iota(jnp.int32, mask_buf.shape, 1)
    mask_buf[...] = jnp.where(place < len_ref[0], 0.0, NEGATIVE)
    new_k[...] = jnp.zeros(new_k.shape, new_k.dtype)
    new_v[...] = jnp.zeros(new_v.shape, new_v.dtype)

    gather_pass_on(0, 0)
    project(0, 0)
    gather_pass_on(0, 1)
    attend(0, 0)
    mix(0, 0)
    project(0, 1)
    combine(0, 0)
    attend(0, 1)
    finish_first(0)
    mix(0, 1)
    enter(0)
    combine(0, 1)
    gather_pass_on(1, 0)
    finish_first(1)
    enter(1)
    project(1, 0)
    gather_pass_on(1, 1)
    attend(1, 0)
    mix(1, 0)
    project(1, 1)
    combine(1, 0)
    attend(1, 1)
    finish_second(0)
    mix(1, 1)
    combine(1, 1)
    finish_second(1)

    kept_back = list(forward_copies.values())
    for made in copies:
        if not any(made is other for other in kept_back):
            made.wait_send()

    @pl.when(seg < seg_count - 1)
    def _():
        for made in kept_back:
            made.wait_send()


def fused(slices, new_slice, norm_gain, w_query, w_keyval, w_out, cached_rows, lengths):
    rows, features = slices.shape
    head_count = lax.axis_size("head")
    row_chunks = 2
    chunk = rows // row_chunks
    half = chunk // 2
    width = head_count * features
    query_columns = w_query.shape[2]
    local_heads = query_columns // HD
    cached = cached_rows.shape[1]
    half_dim = HD // 2
    exponent = jnp.arange(half_dim, dtype=jnp.float32) * (2.0 / HD)
    inverse = jnp.power(jnp.float32(ROPE_BASE), -exponent)
    positions = (lengths[0] + jnp.arange(2 * rows, dtype=jnp.int32)).astype(jnp.float32)
    angles = positions[:, None] * inverse[None, :]
    cosine = jnp.cos(angles)
    sine = jnp.sin(angles)
    cosines = jnp.concatenate([cosine, cosine], axis=1)
    sines = jnp.concatenate([-sine, sine], axis=1)
    vmem = pl.BlockSpec(memory_space=pltpu.VMEM)
    anywhere = pl.BlockSpec(memory_space=pl.ANY)
    narrow = jnp.bfloat16
    wide = jnp.float32
    copy_count = 12 * 2 * row_chunks + row_chunks
    flops = 4 * rows * width * (w_query.shape[2] * 2 + w_keyval.shape[2]) + 8 * rows * local_heads * HD * cached
    return pl.pallas_call(
        functools.partial(exchange_kernel, row_chunks),
        out_shape=(jax.ShapeDtypeStruct((rows, features), wide),) * 2,
        in_specs=[vmem] * 5 + [pl.BlockSpec(memory_space=pltpu.SMEM)] + [anywhere] * 4,
        out_specs=(vmem, vmem),
        scratch_shapes=[
            pltpu.VMEM(w_query.shape[1:], narrow),
            pltpu.VMEM(w_keyval.shape[1:], narrow),
            pltpu.VMEM(w_out.shape[1:], narrow),
            pltpu.VMEM(cached_rows.shape[1:], narrow),
            pltpu.VMEM((2, head_count, rows, features), narrow),
            pltpu.VMEM((chunk, width), narrow),
            pltpu.VMEM((local_heads * chunk, HD), narrow),
            pltpu.VMEM((local_heads * chunk, cached), wide),
            pltpu.VMEM((1, cached), wide),
            pltpu.VMEM((2, rows, HD), narrow),
            pltpu.VMEM((2, rows, HD), narrow),
            pltpu.VMEM((chunk, query_columns), narrow),
            pltpu.VMEM((2, rows, features), narrow),
            pltpu.VMEM((2, rows, features), narrow),
            pltpu.VMEM((2, rows, features), narrow),
            pltpu.VMEM((row_chunks, half, features), wide),
            pltpu.VMEM((row_chunks, half, features), wide),
            pltpu.VMEM((rows, features), wide),
            pltpu.VMEM((2, row_chunks, half, features), narrow),
            pltpu.VMEM((2, row_chunks, half, features), narrow),
            pltpu.VMEM((2, rows, features), narrow),
            pltpu.VMEM((2, rows, features), narrow),
            pltpu.VMEM((rows, features), narrow),
            pltpu.SemaphoreType.DMA((4,)),
            pltpu.SemaphoreType.DMA((copy_count,)),
            pltpu.SemaphoreType.DMA((copy_count,)),
        ],
        compiler_params=pltpu.CompilerParams(
            collective_id=0, has_side_effects=True, vmem_limit_bytes=56 * 1024 * 1024
        ),
        cost_estimate=pl.CostEstimate(
            flops=flops, bytes_accessed=2 * (w_query.size + w_keyval.size + w_out.size + cached_rows.size),
            transcendentals=2 * rows * local_heads * cached,
        ),
    )(slices, new_slice, norm_gain, cosines, sines, lengths, w_query, w_keyval, w_out, cached_rows)


def solution(mesh):
    placed = (
        P("segment", "head"),
        P(None, "head"),
        P("segment", None),
        P("segment", None, "head"),
        P("segment", None, "head"),
        P("segment", "head", None),
        P("segment", "head", None),
        P("segment"),
    )
    square = mesh.shape["head"] == KVH
    return jax.shard_map(
        fused if square else local,
        mesh=mesh,
        in_specs=placed,
        out_specs=(P("segment", "head"), P("segment", "head")),
        check_vma=False,
    )
```
